32 devices in a mesh: section: 2 (over core), dp: 16 (over z, y, x).
Axes of the slice: x: 2, y: 2, z: 4, core: 2. Of those that a mesh axis runs over, the one named last changes fastest.
Arguments:
- inputs: bfloat16 [2, 3072, 1024], P(None, 'dp', 'section'), may hold values from -6 to 6
- lengths: int32 [2, 16, 5], P(None, 'dp'), may hold values from 1 to 64, 128 in all within a row
- labels: int32 [2, 32], replicated, may hold values from 0 to 63, as said below
- w_qkv: float32 [2, 1024, 3072], P('section', 'dp'), may hold values from -0.1875 to 0.1875
- w_out: float32 [2, 1024, 1024], P('section', 'dp'), may hold values from -0.5 to 0.5
- w_up: float32 [2, 1024, 4096], P('section', 'dp'), may hold values from -0.1875 to 0.1875
- w_down: float32 [2, 4096, 1024], P('section', 'dp'), may hold values from -0.125 to 0.125
- ln_gain: float32 [2, 2, 1024], P('section', None, 'dp'), may hold values from 0.5 to 1.5
- ln_bias: float32 [2, 2, 1024], P('section', None, 'dp'), may hold values from -2 to 2
- head_a: float32 [1024, 128], P(('section', 'dp')), may hold values from -0.1875 to 0.1875
- head_b: float32 [1024, 96], P(('section', 'dp')), may hold values from -0.1875 to 0.1875
- head_c: float32 [1024, 64], P(('section', 'dp')), may hold values from -0.1875 to 0.1875
Outputs:
- loss: float32 [2, 16, 2], P(None, 'dp', 'section')
- grad_inputs: float32 [2, 3072, 1024], P(None, 'dp', 'section')
- grad_qkv: float32 [2, 1024, 3072], P('section', 'dp')
- grad_out: float32 [2, 1024, 1024], P('section', 'dp')
- grad_up: float32 [2, 1024, 4096], P('section', 'dp')
- grad_down: float32 [2, 4096, 1024], P('section', 'dp')
- grad_gain: float32 [2, 2, 1024], P('section', None, 'dp')
- grad_bias: float32 [2, 2, 1024], P('section', None, 'dp')
- grad_head_a: float32 [1024, 128], P(('section', 'dp'))
- grad_head_b: float32 [1024, 96], P(('section', 'dp'))
- grad_head_c: float32 [1024, 64], P(('section', 'dp'))
The draws below stay inside these ranges and needn't reach their ends.
Inputs may be any that keep to these rules, and one draw needn't show every extreme that they name: Each row's 4 document lengths and its final pad length sum to 128; every entry is at least 1. `labels`: global document numbers of the same micro-batch.
All inputs are finite; a program needn't handle non-finite values.
Results may differ from the reference program's by a relative error of at most 0.017.
The reference program's roundings to bfloat16 on the way count: a program that leaves them out, or rounds other values in their place, can miss the bound.
Values may be sent and summed in bfloat16 or wider, within the bound.
No kernel may reach another device: no remote copies, remote signals or barrier semaphores. Data moves between devices by JAX's collectives and lax.ppermute only.
A program may use at most 192 MiB of HBM per device.

```python
import math
import jax
import jax.numpy as jnp
import numpy as np
from jax import lax

D = 1024
HEADS = 16
DH = 64
FF = 4096
EA = 128
EB = 96
EC = 64
ROW = 128
NSEG = 4
QDEV = 2
QLEN = 32
MICRO = 2
TOK_DEV = 192
TOKENS = 3072
QUERIES = 32
NDOCS = 64
N_DP = 16


def draw_labels(key, part):
    key = jax.random.fold_in(key, 11)
    drawn = jax.random.randint(key, (MICRO, QUERIES), 0, NDOCS, dtype=jnp.int32)
    lower_key, upper_key = jax.random.split(jax.random.fold_in(key, 1))
    spot_lower = jax.random.randint(lower_key, (MICRO, 1), 0, QUERIES // 2, dtype=jnp.int32)
    spot_upper = jax.random.randint(upper_key, (MICRO, 1), QUERIES // 2, QUERIES, dtype=jnp.int32)
    places = jnp.arange(QUERIES, dtype=jnp.int32)[None, :]
    drawn = jnp.where(places == spot_lower, 0, drawn)
    drawn = jnp.where(places == spot_upper, NDOCS - 1, drawn)
    return drawn.astype(jnp.int32)


def block_scale(stream_key, extent, pieces, smallest, high):
    def one(axis_at, parts):
        heights = jax.random.uniform(jax.random.fold_in(jax.random.fold_in(stream_key, 6), axis_at), (parts,), jnp.float32, smallest / len(pieces), high / len(pieces))
        return jnp.repeat(jnp.exp(heights), extent[axis_at] // parts).reshape((-1,) + (1,) * (len(extent) - axis_at - 1))

    factor_of = one(*pieces[0])
    for cut in pieces[1:]:
        factor_of = factor_of * one(*cut)
    return factor_of


def profile(number_of, total, reach, lean):
    loads = [(1 << 20) // math.isqrt(standing ** lean) + 1 for standing in range(2, number_of + 1)]
    rest, counts = total - reach - (number_of - 1), [1] * (number_of - 1)
    while rest > 0:
        movable = [i for i in range(number_of - 1) if counts[i] < reach]
        mass, budget = sum([loads[i] for i in movable]), rest
        for i in movable:
            addition = min(reach - counts[i], max(1, budget * loads[i] // mass), rest)
            counts[i] = counts[i] + addition
            rest = rest - addition
    return np.array([reach] + counts)


def ragged_sizes(own_key, count, total, reach, slope):
    if count == 2:
        one = jax.random.randint(own_key, (), max(1, total - reach), min(reach, total - 1) + 1)
        return jnp.stack([one, total - one])
    tallies = jnp.asarray(profile(count, total, reach, slope), jnp.int32)
    twos = (count - 1) // 2
    giver, taker = tallies[1:1 + 2 * twos:2], tallies[2:2 + 2 * twos:2]
    margin = jnp.minimum(giver - 1, reach - taker)
    shifted = jax.random.randint(jax.random.fold_in(own_key, 1), (twos,), 0, 1 << 20) % (margin + 1)
    tallies = tallies.at[1:1 + 2 * twos:2].set(giver - shifted).at[2:2 + 2 * twos:2].set(taker + shifted)
    return tallies[jax.random.permutation(jax.random.fold_in(own_key, 2), count)]


def bell_draw(stream_key, extent, spread, bound, cuts=(), kind=jnp.bfloat16):
    values = spread * jax.random.normal(stream_key, extent, jnp.float32)
    if cuts:
        values = values * block_scale(stream_key, extent, cuts, -0.22, 0.18)
    return jnp.clip(values, -bound, bound).astype(kind)


def setup_inputs(seed: int = 0) -> dict:
    splits = jax.random.split(jax.random.key(seed), 13)
    inputs = bell_draw(splits[0], (MICRO, TOKENS, D), 1.0, 6.0, ((1, 16), (2, 2)))
    lengths = jax.vmap(lambda own: ragged_sizes(own, NSEG + 1, ROW, ROW // 2, 1))(jax.random.split(splits[1], MICRO * N_DP)).reshape((MICRO, N_DP, NSEG + 1)).astype(jnp.int32)
    labels = draw_labels(jax.random.fold_in(splits[12], 71), 0)
    w_qkv = bell_draw(splits[3], (2, D, 3 * D), D ** -0.5, 0.1875, ((0, 2), (1, 16)), jnp.float32)
    w_out = bell_draw(splits[4], (2, D, D), (D // 8) ** -0.5, 0.5, ((0, 2), (1, 16)), jnp.float32)
    w_up = bell_draw(splits[5], (2, D, FF), D ** -0.5, 0.1875, ((0, 2), (1, 16)), jnp.float32)
    w_down = bell_draw(splits[6], (2, FF, D), (FF // 2) ** -0.5, 0.125, ((0, 2), (1, 16)), jnp.float32)
    ln_gain = jnp.clip(1.0 + 0.1 * jax.random.normal(splits[7], (2, 2, D), jnp.float32), 0.5, 1.5)
    ln_bias = bell_draw(splits[8], (2, 2, D), 0.3, 2.0, ((0, 2), (2, 16)), jnp.float32)
    head_a = bell_draw(splits[9], (D, EA), D ** -0.5, 0.1875, ((0, 32),), jnp.float32)
    head_b = bell_draw(splits[10], (D, EB), D ** -0.5, 0.1875, ((0, 32),), jnp.float32)
    head_c = bell_draw(splits[11], (D, EC), D ** -0.5, 0.1875, ((0, 32),), jnp.float32)
    return dict(inputs=inputs, lengths=lengths, labels=labels, w_qkv=w_qkv, w_out=w_out, w_up=w_up, w_down=w_down, ln_gain=ln_gain, ln_bias=ln_bias, head_a=head_a, head_b=head_b, head_c=head_c)


ln_eps = 1e-05
norm_eps = 1e-06
sharpness = 16.0
masked_score = -1000000000.0
highest = lax.Precision.HIGHEST

@jax.custom_vjp
def low(v):
    return lax.optimization_barrier(v.astype(jnp.bfloat16)).astype(jnp.float32)

@jax.custom_vjp
def low_back(v):
    return v

def low_keep(v):
    return (low(v), None)

def low_pass(kept, grad):
    return (grad,)

def back_keep(v):
    return (v, None)

def back_low(kept, grad):
    return (low(grad),)
low.defvjp(low_keep, low_pass)
low_back.defvjp(back_keep, back_low)

def matmul(left, right):
    return jnp.dot(left, right, precision=highest, preferred_element_type=jnp.float32)

def layout(row_lengths):
    ends = jnp.cumsum(row_lengths).astype(jnp.int32)
    starts = (ends - row_lengths).astype(jnp.int32)
    places = jnp.arange(ROW, dtype=jnp.int32)
    doc_seg = lax.optimization_barrier(jnp.sum((places[:, None] >= ends[None, :]).astype(jnp.int32), axis=1)).astype(jnp.int32)
    owners = doc_seg[:, None] == jnp.arange(NSEG + 1, dtype=jnp.int32)[None, :]
    doc_pos = places - lax.optimization_barrier(jnp.sum(jnp.where(owners, starts[None, :], 0), axis=1)).astype(jnp.int32)
    query_places = jnp.arange(QDEV * QLEN, dtype=jnp.int32)
    query_seg = NSEG + 1 + query_places // QLEN
    query_pos = query_places % QLEN
    segment_ids = jnp.concatenate([doc_seg, query_seg.astype(jnp.int32)]).astype(jnp.int32)
    positions = jnp.concatenate([doc_pos, query_pos.astype(jnp.int32)]).astype(jnp.int32)
    return (segment_ids, positions)

def rotary(positions):
    half_dim = DH // 2
    freqs = jnp.exp(jnp.arange(half_dim, dtype=jnp.float32) * (-math.log(10000.0) / half_dim))
    angles = positions.astype(jnp.float32)[..., None] * freqs
    cosine = jnp.cos(angles)
    sine = jnp.sin(angles)
    return (jnp.concatenate([cosine, cosine], -1), jnp.concatenate([sine, sine], -1))

def rope(values, cosine, sine):
    half_dim = values.shape[-1] // 2
    turned = jnp.concatenate([-values[..., half_dim:], values[..., :half_dim]], -1)
    return values * cosine[..., None, :] + turned * sine[..., None, :]

def layer_norm(values, gain, bias):
    centre = values - lax.optimization_barrier(jnp.mean(values, -1, keepdims=True))
    variance = lax.optimization_barrier(jnp.mean(centre * centre, -1, keepdims=True))
    return centre * lax.rsqrt(variance + ln_eps) * gain + bias

def attend_row(block):
    query_row, key_row, value_row, seg_row = block
    scores = low_back(jnp.einsum('thd,uhd->htu', query_row, key_row, precision=highest) * 0.125)
    same_doc = seg_row[:, None] == seg_row[None, :]
    scores = jnp.where(same_doc[None], scores, masked_score)
    weights = jax.nn.softmax(scores, axis=-1)
    return jnp.einsum('htu,uhd->thd', low(weights), value_row, precision=highest)

def layer(hidden, w_qkv, w_out, w_up, w_down, gains, biases, segments, cosine, sine):
    mixed_in = low_back(matmul(hidden, low(w_qkv))).reshape(N_DP, TOK_DEV, 3, HEADS, DH)
    queries = low(rope(mixed_in[:, :, 0], cosine, sine))
    keys = low(rope(mixed_in[:, :, 1], cosine, sine))
    values = low(mixed_in[:, :, 2])
    attended = lax.map(jax.checkpoint(attend_row), (queries, keys, values, segments))
    attended = low_back(low(attended.reshape(N_DP * TOK_DEV, D)))
    branch = low_back(matmul(attended, low(w_out)))
    gains = low(gains)
    biases = low(biases)
    middle = layer_norm(hidden + branch, gains[0], biases[0])
    raised = low_back(matmul(low(middle), low(w_up)))
    active = low(jax.nn.gelu(raised, approximate=False))
    lowered = low_back(matmul(active, low(w_down)))
    return layer_norm(middle + lowered, gains[1], biases[1])

def head_losses(final, heads, segments, labels_row):
    flat_rows = low(final)
    doc_seg = segments[:, :ROW]
    members = (doc_seg[..., None] == jnp.arange(NSEG, dtype=jnp.int32)).astype(jnp.float32)
    docs_index = jnp.arange(NDOCS, dtype=jnp.int32)
    per_query = jnp.zeros((QUERIES,), jnp.float32)
    for w_head in heads:
        head_width = w_head.shape[1]
        embedded = low_back(matmul(flat_rows, low(w_head)))
        unit_list = low(embedded * lax.rsqrt(lax.optimization_barrier(jnp.sum(embedded * embedded, -1, keepdims=True)) + norm_eps))
        unit_list = unit_list.reshape(N_DP, TOK_DEV, head_width)
        all_queries = unit_list[:, ROW:].reshape(QUERIES * QLEN, head_width)

        def row_logits(row_pair, all_queries=all_queries):
            doc_units, member = row_pair
            similar = low_back(matmul(all_queries, doc_units.T))
            masses = matmul(jnp.exp(sharpness * similar), member)
            token_score = jnp.log(masses) / sharpness
            return lax.optimization_barrier(jnp.sum(token_score.reshape(QUERIES, QLEN, NSEG), axis=1))
        logits = lax.map(jax.checkpoint(row_logits), (unit_list[:, :ROW], members))
        logits = jnp.transpose(logits, (1, 0, 2)).reshape(QUERIES, NDOCS)
        picked = lax.optimization_barrier(jnp.sum(jnp.where(docs_index[None, :] == labels_row[:, None], logits, 0.0), axis=1))
        per_query = per_query + jax.nn.logsumexp(logits, axis=1) - picked
    return per_query

def reference(inputs, lengths, labels, w_qkv, w_out, w_up, w_down, ln_gain, ln_bias, head_a, head_b, head_c):
    segments, positions = jax.vmap(jax.vmap(layout))(lengths)
    cosine, sine = rotary(positions)

    def objective(hidden_in, qkv_all, out_all, up_all, down_all, gain_all, bias_all, head_one, head_two, head_three):
        results = []
        for micro_idx in range(MICRO):
            hidden = hidden_in[micro_idx]
            for depth in range(2):
                hidden = jax.checkpoint(layer)(hidden, qkv_all[depth], out_all[depth], up_all[depth], down_all[depth], gain_all[depth], bias_all[depth], segments[micro_idx], cosine[micro_idx], sine[micro_idx])
                if depth == 0:
                    hidden = low_back(low(hidden))
            results.append(head_losses(hidden, (head_one, head_two, head_three), segments[micro_idx], labels[micro_idx]))
        per_query = jnp.stack(results)
        return (jnp.sum(per_query), per_query)
    primals = tuple((array_in.astype(jnp.float32) for array_in in (inputs, w_qkv, w_out, w_up, w_down, ln_gain, ln_bias, head_a, head_b, head_c)))
    total, pull_back, per_query = jax.vjp(objective, *primals, has_aux=True)
    grads = pull_back(jnp.ones_like(total))
    return (per_query.reshape(MICRO, N_DP, QDEV), grads[0], grads[1], grads[2], grads[3], grads[4], grads[5], grads[6], grads[7], grads[8], grads[9])
```

```python
import math

import jax
import jax.numpy as jnp
from jax import lax
from jax.sharding import PartitionSpec as P

D = 1024
DH = 64
ROW = 128
NSEG = 4
QDEV = 2
QLEN = 32
WIDTHS = (128, 96, 64)

ln_eps = 1e-05
norm_eps = 1e-06
sharpness = 16.0
masked_score = -1000000000.0
highest = lax.Precision.HIGHEST
bf16 = jnp.bfloat16
f32 = jnp.float32


def factors(count, ways):
    sizes = [1] * ways
    left = count
    while left > 1:
        at = min(range(ways), key=lambda i: (sizes[i], i))
        sizes[at] *= 2
        left //= 2
    return tuple(sorted(sizes, reverse=True))


def route(dims, axis, step):
    stride = math.prod(dims[axis + 1 :])
    pairs = []
    for source in range(math.prod(dims)):
        digit = source // stride % dims[axis]
        pairs.append((source, source + ((digit ^ step) - digit) * stride))
    return pairs


def digits_of(dims):
    index = lax.axis_index("dp")
    return [index // math.prod(dims[a + 1 :]) % dims[a] for a in range(len(dims))]


def gather_blocks(shard, dims, order):
    digits = digits_of(dims)
    have = shard.reshape((1,) * len(dims) + shard.shape)
    for axis in order:
        count = dims[axis]
        if count == 1:
            continue
        parts = [have] + [
            lax.ppermute(have, "dp", route(dims, axis, k)) for k in range(1, count)
        ]
        if count == 2:
            have = jnp.where(
                digits[axis] == 0,
                jnp.concatenate(parts, axis),
                jnp.concatenate(parts[::-1], axis),
            )
        else:
            stacked = jnp.concatenate(parts, axis)
            have = jnp.concatenate(
                [
                    lax.dynamic_slice_in_dim(stacked, digits[axis] ^ j, 1, axis)
                    for j in range(count)
                ],
                axis,
            )
    return have


def scatter_blocks(total, dims, order, wire):
    digits = digits_of(dims)
    for axis in order:
        count = dims[axis]
        if count == 1:
            continue
        own = lax.dynamic_slice_in_dim(total, digits[axis], 1, axis)
        for k in range(1, count):
            part = lax.dynamic_slice_in_dim(total, digits[axis] ^ k, 1, axis).astype(wire)
            own = own + lax.ppermute(part, "dp", route(dims, axis, k)).astype(f32)
        total = own
    return total.reshape(total.shape[len(dims) :])


def swap(value):
    return lax.ppermute(value, "section", [(0, 1), (1, 0)])


def one_way(value, source):
    return lax.ppermute(value, "section", [(source, 1 - source)])


def by_core(is_first, mine, other, axis):
    return jnp.where(
        is_first,
        jnp.concatenate([mine, other], axis),
        jnp.concatenate([other, mine], axis),
    )


def layout(row_lengths):
    ends = jnp.cumsum(row_lengths)
    starts = ends - row_lengths
    places = jnp.arange(ROW, dtype=jnp.int32)
    doc_seg = jnp.sum((places[:, None] >= ends[None, :]).astype(jnp.int32), axis=1)
    owners = doc_seg[:, None] == jnp.arange(NSEG + 1, dtype=jnp.int32)[None, :]
    doc_pos = places - jnp.sum(jnp.where(owners, starts[None, :], 0), axis=1)
    query_places = jnp.arange(QDEV * QLEN, dtype=jnp.int32)
    query_seg = NSEG + 1 + query_places // QLEN
    query_pos = query_places % QLEN
    segment_ids = jnp.concatenate([doc_seg, query_seg])
    positions = jnp.concatenate([doc_pos, query_pos])
    return (segment_ids, positions)


def rotary(positions):
    half_dim = DH // 2
    freqs = jnp.exp(jnp.arange(half_dim, dtype=f32) * (-math.log(10000.0) / half_dim))
    angles = positions.astype(f32)[..., None] * freqs
    cosine = jnp.cos(angles)
    sine = jnp.sin(angles)
    return (jnp.concatenate([cosine, cosine], -1), jnp.concatenate([sine, sine], -1))


def rope(values, cosine, sine):
    half_dim = values.shape[-1] // 2
    turned = jnp.concatenate([-values[..., half_dim:], values[..., :half_dim]], -1)
    return values * cosine[..., None, :] + turned * sine[..., None, :]


def rope_back(grads, cosine, sine):
    half_dim = grads.shape[-1] // 2
    scaled = grads * sine[..., None, :]
    turned = jnp.concatenate([scaled[..., half_dim:], -scaled[..., :half_dim]], -1)
    return grads * cosine[..., None, :] + turned


def normalize(values):
    centre = values - jnp.mean(values, -1, keepdims=True)
    scale = lax.rsqrt(jnp.mean(centre * centre, -1, keepdims=True) + ln_eps)
    return centre * scale, scale


def normalize_back(grad, gain, normal, scale):
    inner = grad * gain
    mean_inner = jnp.mean(inner, -1, keepdims=True)
    mean_mixed = jnp.mean(inner * normal, -1, keepdims=True)
    return (
        scale * (inner - mean_inner - normal * mean_mixed),
        jnp.sum(grad * normal, 0),
        jnp.sum(grad, 0),
    )


def gelu(values):
    return 0.5 * values * (1.0 + lax.erf(values * math.sqrt(0.5)))


def gelu_slope(values):
    density = jnp.exp(-0.5 * values * values) * (1.0 / math.sqrt(2.0 * math.pi))
    return 0.5 * (1.0 + lax.erf(values * math.sqrt(0.5))) + values * density


def dot_plain(left, right):
    return jnp.dot(left, right, preferred_element_type=f32)


def dot_left_t(left, right):
    return lax.dot_general(left, right, (((0,), (0,)), ((), ())), preferred_element_type=f32)


def dot_right_t(left, right):
    return lax.dot_general(left, right, (((1,), (1,)), ((), ())), preferred_element_type=f32)


def masked_scores(q_rot, k_rot, same):
    scores = jnp.einsum("mthd,muhd->mhtu", q_rot, k_rot, preferred_element_type=f32) * 0.125
    return jnp.where(same[:, None], scores, masked_score)


def softmax_rows(scores):
    raised = jnp.exp(scores - jnp.max(scores, -1, keepdims=True))
    return raised / jnp.sum(raised, -1, keepdims=True)


def layer_ahead(entry, weights, norms, where):
    w_qkv, w_out, w_up, w_down = weights
    gains, biases = norms
    is_first, same, cosine, sine = where
    rows = entry.shape[0] // 2
    mixed = dot_plain(entry, w_qkv)
    width = mixed.shape[1] // 3

    def heads_of(values):
        return values.reshape(2, rows, width // DH, DH)

    q_rot = rope(heads_of(mixed[:, :width]), cosine, sine).astype(bf16)
    k_rot = rope(heads_of(mixed[:, width : 2 * width]), cosine, sine).astype(bf16)
    v_low = heads_of(mixed[:, 2 * width :]).astype(bf16)
    soft = softmax_rows(masked_scores(q_rot, k_rot, same))
    attended = jnp.einsum("mhtu,muhd->mthd", soft.astype(bf16), v_low, preferred_element_type=f32)
    o_half = attended.reshape(2 * rows, width).astype(bf16)
    o_other = swap(jnp.concatenate([o_half[rows:], o_half[:rows]], 0))
    o_full = by_core(is_first, o_half, o_other, 1)
    branch = dot_plain(o_full[:rows], w_out)
    normal_one, scale_one = normalize(entry[:rows].astype(f32) + branch)
    middle = normal_one * gains[0] + biases[0]
    middle_low = middle.astype(bf16)
    middle_both = jnp.concatenate([middle_low, swap(middle_low)], 0)
    raised = dot_plain(middle_both, w_up)
    active = gelu(raised).astype(bf16)
    lowered = dot_plain(active, w_down)
    lowered = lowered[:rows] + swap(lowered[rows:])
    normal_two, scale_two = normalize(middle + lowered)
    result = normal_two * gains[1] + biases[1]
    kept = (entry, q_rot, k_rot, v_low, o_full, normal_one, scale_one, middle_both, raised, active)
    return result, kept + (normal_two, scale_two)


def layer_back(grad, kept, weights, norms, where, block_rows):
    entry, q_rot, k_rot, v_low, o_full, normal_one, scale_one, middle_both, raised, active = kept[:10]
    normal_two, scale_two = kept[10:]
    w_qkv, w_out, w_up, w_down = weights
    gains, _ = norms
    is_first, same, cosine, sine = where
    rows = grad.shape[0]
    d_two, d_gain_two, d_bias_two = normalize_back(grad, gains[1], normal_two, scale_two)
    d_low = d_two.astype(bf16)
    d_lowered = jnp.concatenate([d_low, swap(d_low)], 0)
    g_down = dot_left_t(active, d_lowered)
    d_active = dot_right_t(d_lowered, w_down)
    d_raised = (d_active * gelu_slope(raised)).astype(bf16)
    g_up = dot_left_t(middle_both, d_raised)
    d_middle = dot_right_t(d_raised, w_up)
    d_middle = d_two + d_middle[:rows] + swap(d_middle[rows:])
    d_one, d_gain_one, d_bias_one = normalize_back(d_middle, gains[0], normal_one, scale_one)
    d_low = d_one.astype(bf16)
    d_branch = jnp.concatenate([d_low, swap(d_low)], 0)
    half = D // 2
    g_out = dot_left_t(o_full, jnp.where(is_first, d_branch[:, :half], d_branch[:, half:]))
    w_mine = jnp.where(is_first, w_out[:half], w_out[half:])
    d_attended = dot_right_t(d_branch, w_mine).astype(bf16)
    d_attended = d_attended.reshape(v_low.shape)
    soft = softmax_rows(masked_scores(q_rot, k_rot, same))
    d_soft = jnp.einsum("mthd,muhd->mhtu", d_attended, v_low, preferred_element_type=f32)
    d_value = jnp.einsum(
        "mhtu,mthd->muhd", soft.astype(bf16), d_attended, preferred_element_type=f32
    )
    inner = jnp.sum(soft * d_soft, -1, keepdims=True)
    d_scores = (soft * (d_soft - inner)).astype(bf16)
    d_query = jnp.einsum("mhtu,muhd->mthd", d_scores, k_rot, preferred_element_type=f32) * 0.125
    d_key = jnp.einsum("mhtu,mthd->muhd", d_scores, q_rot, preferred_element_type=f32) * 0.125
    d_mixed = jnp.concatenate(
        [
            part.reshape(2 * rows, -1).astype(bf16)
            for part in (
                rope_back(d_query, cosine, sine),
                rope_back(d_key, cosine, sine),
                d_value,
            )
        ],
        axis=1,
    )
    g_qkv = dot_left_t(entry, d_mixed)
    d_entry = dot_right_t(d_mixed, w_qkv)
    norm_grads = (d_gain_one, d_gain_two, d_bias_one, d_bias_two)
    return d_one, d_entry, (g_qkv, g_out, g_up, g_down), norm_grads


def head_pass(final, heads, segments, labels_row, small):
    dp_index = lax.axis_index("dp")
    flat_rows = final.astype(bf16)
    cuts = [sum(WIDTHS[:k]) for k in range(4)]
    spans = [(cuts[k], cuts[k + 1]) for k in range(3)]
    member = (segments[:ROW, None] == jnp.arange(NSEG, dtype=jnp.int32)[None, :]).astype(f32)
    embedded = dot_plain(flat_rows, heads)
    inverse = [
        lax.rsqrt(jnp.sum(jnp.square(embedded[:, a:b]), -1, keepdims=True) + norm_eps)
        for a, b in spans
    ]
    exact = [embedded[:, a:b] * inverse[k] for k, (a, b) in enumerate(spans)]
    units = jnp.concatenate(exact, 1).astype(bf16)
    everyone = gather_blocks(units[ROW:], small, range(len(small)))
    everyone = everyone.reshape(-1, units.shape[1])
    exponents = []
    masses = []
    local = []
    for a, b in spans:
        similar = dot_right_t(units[:ROW, a:b], everyone[:, a:b])
        expo = jnp.exp(sharpness * similar)
        mass = lax.dot_general(member, expo, (((0,), (0,)), ((), ())), precision=highest)
        exponents.append(expo)
        masses.append(mass)
        local.append(jnp.sum((jnp.log(mass) / sharpness).reshape(NSEG, -1, QLEN), -1))
    local = jnp.stack(local)
    logits = gather_blocks(local, small, range(len(small)))
    logits = jnp.moveaxis(logits.reshape((-1,) + local.shape), 0, 1)
    logits = logits.reshape(3, -1, local.shape[2])
    label_hot = jnp.arange(logits.shape[1], dtype=jnp.int32)[:, None] == labels_row[None, :]
    label_hot = label_hot.astype(f32)
    peak = jnp.max(logits, 1, keepdims=True)
    spread = jnp.exp(logits - peak)
    totals = jnp.sum(spread, 1, keepdims=True)
    per_query = jnp.sum(peak[:, 0] + jnp.log(totals[:, 0]) - jnp.sum(logits * label_hot, 1), 0)
    own_losses = lax.dynamic_slice_in_dim(per_query, dp_index * QDEV, QDEV)
    d_logits = spread / totals - label_hot
    d_local = lax.dynamic_slice_in_dim(d_logits, dp_index * NSEG, NSEG, 1)
    d_queries = []
    d_docs = []
    for k, (a, b) in enumerate(spans):
        d_mass = jnp.repeat(d_local[k], QLEN, axis=1) / (sharpness * masses[k])
        d_expo = jnp.dot(member, d_mass, precision=highest)
        d_similar = (d_expo * exponents[k] * sharpness).astype(bf16)
        d_queries.append(dot_left_t(d_similar, units[:ROW, a:b]))
        d_docs.append(dot_plain(d_similar, everyone[:, a:b]))
    d_queries = jnp.concatenate(d_queries, 1)
    d_queries = d_queries.reshape(small + (-1,) + d_queries.shape[1:])
    back = scatter_blocks(d_queries, small, range(len(small))[::-1], bf16)
    d_unit = jnp.concatenate([jnp.concatenate(d_docs, 1), back], 0)
    d_embedded = []
    for k, (a, b) in enumerate(spans):
        along = jnp.sum(d_unit[:, a:b] * exact[k], -1, keepdims=True)
        d_embedded.append((d_unit[:, a:b] - exact[k] * along) * inverse[k])
    d_embedded = jnp.concatenate(d_embedded, 1).astype(bf16)
    return own_losses, dot_right_t(d_embedded, heads), dot_left_t(flat_rows, d_embedded)


def halves_of(mine, is_first):
    kept = jnp.where(is_first, mine[0], mine[1])
    other = swap(jnp.where(is_first, mine[1], mine[0]))
    return jnp.where(is_first, kept, other), jnp.where(is_first, other, kept)


def on_device(
    inputs, lengths, labels, w_qkv, w_out, w_up, w_down, ln_gain, ln_bias, head_a, head_b, head_c
):
    peers = lax.axis_size("dp")
    dims = factors(peers, 3)
    small = factors(peers, 2)
    is_first = lax.axis_index("section") == 0
    rows = inputs.shape[1]
    block = w_qkv.shape[1]
    unit_block = w_down.shape[1] // 2

    qkv_half = w_qkv[0].astype(bf16).reshape(block, 3, 2, D // 2)
    qkv_half = jnp.moveaxis(qkv_half, 2, 0).reshape(2, block, -1)
    out_half = jnp.moveaxis(w_out[0].astype(bf16).reshape(block, 2, D // 2), 1, 0)
    up_half = w_up[0].astype(bf16).reshape(block, peers, 2, unit_block)
    up_half = jnp.moveaxis(up_half, 2, 0).reshape(2, block, -1)
    down_half = w_down[0].astype(bf16).reshape(2, unit_block, D)
    attn_parts = halves_of(jnp.concatenate([qkv_half, out_half], 2), is_first)
    up_parts = halves_of(up_half, is_first)
    down_parts = halves_of(down_half, is_first)

    norm_mine = jnp.concatenate([ln_gain[0], ln_bias[0]], 0).astype(bf16)
    norm_both = by_core(is_first, norm_mine[None], swap(norm_mine)[None], 0)
    norms = gather_blocks(norm_both, small, range(len(small)))
    norms = jnp.moveaxis(norms.reshape((peers,) + norm_both.shape), 0, 2)
    norms = norms.reshape(2, 4, D).astype(f32)
    head_mine = jnp.concatenate([head_a, head_b, head_c], 1).astype(bf16)
    head_both = by_core(is_first, head_mine[None], swap(head_mine)[None], 0)
    heads = gather_blocks(head_both, small, range(len(small)))
    heads = jnp.moveaxis(heads.reshape((peers,) + head_both.shape), 0, 1).reshape(D, -1)

    orders = ((0, 1, 2), (0, 2, 1))
    weights = []
    for l in range(2):
        attn = gather_blocks(attn_parts[l], dims, orders[l]).reshape(D, -1)
        up = gather_blocks(up_parts[l], dims, orders[1 - l]).reshape(D, -1)
        down = gather_blocks(down_parts[l], dims, orders[l]).reshape(-1, D)
        out_mine = attn[:, 3 * D // 2 :]
        out = by_core(is_first, out_mine, swap(out_mine), 1)
        weights.append((attn[:, : 3 * D // 2], out, up, down))

    whole = by_core(is_first, inputs, swap(inputs), 2)
    entry = jnp.where(is_first, whole, whole[::-1]).reshape(2 * rows, D)
    own_lengths = jnp.where(is_first, lengths, lengths[::-1])[:, 0]
    segments, positions = jax.vmap(layout)(own_lengths)
    cosine, sine = rotary(positions)
    same = segments[:, :, None] == segments[:, None, :]
    where = (is_first, same, cosine, sine)
    labels_own = jnp.where(is_first, labels[0], labels[1])

    kept = []
    pairs = [((norms[l, 0], norms[l, 1]), (norms[l, 2], norms[l, 3])) for l in range(2)]
    for l in range(2):
        result, saved = layer_ahead(entry, weights[l], pairs[l], where)
        kept.append(saved)
        if l == 0:
            low = result.astype(bf16)
            entry = jnp.concatenate([low, swap(low)], 0)
    losses, grad, g_heads = head_pass(result, heads, segments[0], labels_own, small)

    shards = [None, None]
    norm_grads = [None, None]
    back = ((2, 1, 0), (1, 2, 0))
    for l in (1, 0):
        d_one, d_entry, grads, norm_grads[l] = layer_back(
            grad, kept[l], weights[l], pairs[l], where, block
        )
        g_qkv, g_out, g_up, g_down = grads
        down = scatter_blocks(g_down.reshape(dims + (unit_block, D)), dims, back[l], bf16)
        up = scatter_blocks(g_up.reshape(dims + (block, -1)), dims, back[1 - l], bf16)
        g_attn = jnp.concatenate([g_qkv, g_out], 1)
        if l == 1:
            g_heads = g_heads.reshape(2, D // 2, -1)
            g_mine = jnp.where(is_first, g_heads[0], g_heads[1])
            g_mine = g_mine + swap(jnp.where(is_first, g_heads[1], g_heads[0]))
            g_mine = g_mine.reshape(D, -1)
            g_attn = jnp.concatenate([g_attn, g_mine], 1)
        attn = scatter_blocks(g_attn.reshape(dims + (block, -1)), dims, back[l], bf16)
        if l == 1:
            head_shard = attn[:, 2 * D :].reshape(D // 2 // peers, -1)
        shards[l] = (attn[:, : 3 * D // 2], attn[:, 3 * D // 2 : 2 * D], up, down)
        if l == 1:
            d_entry = d_one + d_entry[:rows] + swap(d_entry[rows:])
            grad = d_entry.astype(bf16).astype(f32)

    partial = jnp.concatenate([d_entry[:rows] + d_one, d_entry[rows:]], 0).reshape(2, rows, D)
    mine = jnp.where(is_first, partial[..., : D // 2], partial[..., D // 2 :])
    other = swap(jnp.where(is_first, partial[..., D // 2 :], partial[..., : D // 2]))
    grad_inputs = mine + other[::-1]
    grad_inputs = jnp.where(is_first, grad_inputs, grad_inputs[::-1])

    owned = []
    for i in range(4):
        from_first = one_way(shards[1][i], 0)
        from_second = one_way(shards[0][i], 1)
        lower = jnp.where(is_first, shards[0][i], from_first)
        upper = jnp.where(is_first, from_second, shards[1][i])
        owned.append((lower, upper))
    grad_qkv = jnp.stack([h.reshape(block, 3, D // 2) for h in owned[0]], 2).reshape(block, 3 * D)
    grad_out = jnp.concatenate(owned[1], 1)
    grad_up = jnp.stack([h.reshape(block, peers, unit_block) for h in owned[2]], 2)
    grad_up = grad_up.reshape(block, -1)
    grad_down = jnp.concatenate(owned[3], 0)

    norm_all = jnp.stack([jnp.stack(norm_grads[l]) for l in range(2)])
    norm_mine = jnp.where(is_first, norm_all[0], norm_all[1])
    norm_mine = norm_mine + swap(jnp.where(is_first, norm_all[1], norm_all[0]))
    norm_mine = jnp.moveaxis(norm_mine.reshape((4,) + small + (-1,)), 0, len(small))
    norm_shard = scatter_blocks(norm_mine, small, range(len(small))[::-1], f32)

    cross = swap(jnp.where(is_first, losses[1], losses[0])[None])[0]
    kept_loss = jnp.where(is_first, losses[0], losses[1])
    loss_out = jnp.where(
        is_first, jnp.stack([kept_loss, cross]), jnp.stack([cross, kept_loss])
    ).reshape(2, 1, 1)
    head_grads = jnp.split(head_shard, [WIDTHS[0], WIDTHS[0] + WIDTHS[1]], axis=1)
    return (
        loss_out,
        grad_inputs,
        grad_qkv[None],
        grad_out[None],
        grad_up[None],
        grad_down[None],
        norm_shard[None, :2],
        norm_shard[None, 2:],
        head_grads[0],
        head_grads[1],
        head_grads[2],
    )


def solution(mesh):
    placed = (
        P(None, "dp", "section"),
        P(None, "dp", None),
        P(),
        P("section", "dp", None),
        P("section", "dp", None),
        P("section", "dp", None),
        P("section", "dp", None),
        P("section", None, "dp"),
        P("section", None, "dp"),
        P(("section", "dp"), None),
        P(("section", "dp"), None),
        P(("section", "dp"), None),
    )
    return jax.shard_map(
        on_device,
        mesh=mesh,
        in_specs=placed,
        out_specs=(
            P(None, "dp", "section"),
            P(None, "dp", "section"),
            P("section", "dp", None),
            P("section", "dp", None),
            P("section", "dp", None),
            P("section", "dp", None),
            P("section", None, "dp"),
            P("section", None, "dp"),
            P(("section", "dp"), None),
            P(("section", "dp"), None),
            P(("section", "dp"), None),
        ),
        check_vma=False,
    )
```
